512 devices in a mesh: rep: 32 (over z_hi, x, core), fsdp: 16 (over y, z_lo).
Axes of the slice: x: 4, y: 4, z: 16 (z_hi: 4, z_lo: 4; z = z_hi * 4 + z_lo), core: 2. Of those that a mesh axis runs over, the one named last changes fastest.
Arguments:
- acts: bfloat16 [32, 3072, 512], P('rep', 'fsdp'), may hold values from -6 to 6
- cotangent: bfloat16 [32, 3072, 4096], P('rep', 'fsdp'), may hold values from -6 to 6
- weight: float32 [32, 512, 4096], P('rep', 'fsdp'), may hold values from -6 to 6
- moment_one: float32 [32, 512, 4096], P('rep', 'fsdp'), may hold values from -2 to 2
- moment_two: float32 [32, 512, 4096], P('rep', 'fsdp'), may hold values from 0.02 to 1
- learn_rate: float32 [1], replicated, may hold values from 0.05 to 0.3
- step_index: int32 [1], replicated, may hold values from 0 to 999
- step_count: int32 [1], replicated, may hold values from 1 to 19
Outputs:
- act_grad: bfloat16 [32, 3072, 512], P('rep', 'fsdp')
- new_weight: float32 [32, 512, 4096], P('rep', 'fsdp')
- new_moment_one: float32 [32, 512, 4096], P('rep', 'fsdp')
- new_moment_two: float32 [32, 512, 4096], P('rep', 'fsdp')
The draws below stay inside these ranges and needn't reach their ends.
Inputs may be any that keep to these rules, and one draw needn't show every extreme that they name: `step_index`: the gossip step; the partner offset is 2 ** (t mod 4). `step_count`: the number of AdamW steps taken, this one included.
All inputs are finite; a program needn't handle non-finite values.
Results may differ from the reference program's by a relative error of at most 0.01.
Values may be sent and summed in bfloat16 or wider, within the bound.
A program may use at most 64 MiB of HBM per device.

```python
import math
import jax
import jax.numpy as jnp
from jax import lax

D = 4096
TOK_DEV = 192
ROWS = 512
TOKENS = 3072
REPLICAS = 32
N_FSDP = 16


def with_spikes(values, key, source, target, parts, factor):
    def block_of(dim):
        return (jnp.arange(values.shape[dim]) // (values.shape[dim] // parts)).reshape((-1,) + (1,) * (values.ndim - 1 - dim))

    near = jax.random.permutation(key, parts)[block_of(target)]
    far = (block_of(target) + parts // 2) % parts
    return jnp.where((block_of(source) == near) | (block_of(source) == far), factor * values, values)


def levels(rng, dims, cuts, smallest, largest):
    def one(axis_at, parts):
        heights = jax.random.uniform(jax.random.fold_in(jax.random.fold_in(rng, 6), axis_at), (parts,), jnp.float32, smallest / len(cuts), largest / len(cuts))
        return jnp.repeat(jnp.exp(heights), dims[axis_at] // parts).reshape((-1,) + (1,) * (len(dims) - axis_at - 1))

    level = one(*cuts[0])
    for cut in cuts[1:]:
        level = level * one(*cut)
    return level


def normal_values(own_key, extent, scale, bound, pieces=(), kind=jnp.bfloat16):
    result = scale * jax.random.normal(own_key, extent, jnp.float32)
    if pieces:
        result = result * levels(own_key, extent, pieces, -0.22, 0.18)
    return jnp.clip(result, -bound, bound).astype(kind)


def heavy_noise(stream_key, shape, spread, reach, pieces, heavy, kind=jnp.bfloat16):
    array = spread * jax.random.normal(stream_key, shape, jnp.float32)
    if pieces:
        array = array * levels(stream_key, shape, pieces, -0.22, 0.18)
    return jnp.clip(with_spikes(array, jax.random.fold_in(stream_key, 3), *heavy), -reach, reach).astype(kind)


def setup_inputs(seed: int = 0) -> dict:
    splits = jax.random.split(jax.random.key(seed), 9)
    return {
        "acts": heavy_noise(splits[0], (REPLICAS, TOKENS, ROWS), 1.0, 6.0, ((0, 32), (1, 16)), (1, 2, 16, 2.0)),
        "cotangent": normal_values(splits[1], (REPLICAS, TOKENS, D), 1.0, 6.0, ((0, 32), (1, 16))),
        "weight": normal_values(splits[2], (REPLICAS, ROWS, D), 1.0, 6.0, ((0, 32), (1, 16)), jnp.float32),
        "moment_one": normal_values(splits[3], (REPLICAS, ROWS, D), 0.3, 2.0, ((0, 32), (1, 16)), jnp.float32),
        "moment_two": jnp.clip(jnp.exp(math.log(1.0) - 3.912023 * jax.random.uniform(splits[4], (REPLICAS, ROWS, D), jnp.float32) ** levels(splits[4], (REPLICAS, ROWS, D), ((0, 32), (1, 16)), -0.2, 0.2)), 0.02, 1.0),
        "learn_rate": jnp.clip(jnp.exp(jax.random.uniform(splits[5], (1,), jnp.float32, math.log(0.05), math.log(0.3))), 0.05, 0.3),
        "step_index": jax.random.randint(splits[6], (1,), 0, 1000).astype(jnp.int32),
        "step_count": jax.random.randint(splits[7], (1,), 1, 20).astype(jnp.int32),
    }


BETA_ONE = 0.9
BETA_TWO = 0.95
EPSILON = 1e-08
DECAY = 0.1
OUT_SCALE = 0.015625

def adamw_update(weight_in, moment_a, moment_b, gradient, learn_value, count_value):
    moment_a_up = BETA_ONE * moment_a + (1.0 - BETA_ONE) * gradient
    moment_b_up = BETA_TWO * moment_b + (1.0 - BETA_TWO) * gradient * gradient
    steps_float = count_value.astype(jnp.float32)
    fix_one = 1.0 - jnp.power(jnp.float32(BETA_ONE), steps_float)
    fix_two = 1.0 - jnp.power(jnp.float32(BETA_TWO), steps_float)
    direction = moment_a_up / fix_one / (jnp.sqrt(moment_b_up / fix_two) + EPSILON) + DECAY * weight_in
    return (weight_in - learn_value * direction, moment_a_up, moment_b_up)

def replica_grads(acts_rep, cotan_rep):
    acts_blocks = acts_rep.reshape(N_FSDP, TOK_DEV, ROWS)
    cotan_blocks = cotan_rep.reshape(N_FSDP, TOK_DEV, D)

    def add_term(total, pair):
        term = OUT_SCALE * jnp.dot(pair[0].T, pair[1], preferred_element_type=jnp.float32)
        rounded = lax.optimization_barrier(term.astype(jnp.bfloat16))
        return (total + rounded.astype(jnp.float32), None)
    total, unused = lax.scan(add_term, jnp.zeros((ROWS, D), jnp.float32), (acts_blocks, cotan_blocks))
    return total

def reference(acts, cotangent, weight, moment_one, moment_two, learn_rate, step_index, step_count):

    def per_replica(items):
        acts_rep, cotan_rep, weight_rep = items
        weight_low = weight_rep.astype(jnp.bfloat16)
        product = OUT_SCALE * jnp.dot(cotan_rep, weight_low.T, preferred_element_type=jnp.float32)
        return (product.astype(jnp.bfloat16), replica_grads(acts_rep, cotan_rep))
    act_grad, gradients = lax.map(per_replica, (acts, cotangent, weight))
    weight_up, moment_a_up, moment_b_up = adamw_update(weight, moment_one, moment_two, gradients, learn_rate[0], step_count[0])
    offset = jnp.left_shift(jnp.int32(1), (step_index[0] % 4).astype(jnp.int32))
    partner = ((jnp.arange(REPLICAS, dtype=jnp.int32) - offset) % REPLICAS).astype(jnp.int32)
    new_weight = 0.5 * (weight_up + weight_up[partner])
    new_moment_one = 0.5 * (moment_a_up + moment_a_up[partner])
    new_moment_two = 0.5 * (moment_b_up + moment_b_up[partner])
    return (act_grad, new_weight, new_moment_one, new_moment_two)
```

```python
from functools import partial

import jax
import jax.numpy as jnp
from jax import lax
from jax.experimental import pallas as pl
from jax.experimental.pallas import tpu as pltpu
from jax.sharding import PartitionSpec as P

BETA_ONE = 0.9
BETA_TWO = 0.95
EPSILON = 1e-08
DECAY = 0.1
OUT_SCALE = 0.015625

MESH = pl.DeviceIdType.MESH
F32 = jnp.float32
BF16 = jnp.bfloat16

N_Y = 4
N_Z = 4
TOK = 192
ROWS = 512
OWN = 32
D = 4096
SLICE = D // N_Y
CHUNKS = 4
CW = SLICE // CHUNKS

CROSSING = {1: ((3, 1),), 2: ((3, None),), 4: ((2, None), (3, None))}


def xor(index, bits):
    low = lax.rem(index, 2)
    high = lax.div(index, 2)
    if bits & 1:
        low = 1 - low
    if bits & 2:
        high = 1 - high
    return high * 2 + low


def gossip_kernel(
    offset,
    par_ref,
    acts_ref,
    cot_ref,
    w_ref,
    ma_ref,
    mb_ref,
    ag_out,
    w_out,
    ma_out,
    mb_out,
    w_low,
    w_full,
    acts_in,
    acts_t,
    cot_in,
    g_send,
    rs_in,
    gb_send,
    gb_in,
    ag_send,
    ag_in,
    go_send,
    go_in,
    relay_in,
    s_w,
    r_w,
    s_acts,
    r_acts,
    s_cot,
    r_cot,
    s_gz,
    r_gz,
    s_rs,
    r_rs,
    s_gb,
    r_gb,
    s_ag,
    r_ag,
    s_go,
    r_go,
    s_rel,
    r_rel,
    s_fwd,
):
    rep = lax.axis_index("rep")
    fs = lax.axis_index("fsdp")
    zh = lax.div(rep, 8)
    xc = lax.rem(rep, 8)
    x = lax.div(xc, 2)
    core = lax.rem(rep, 2)
    y = lax.div(fs, N_Z)
    z = lax.rem(fs, N_Z)

    def at_y(value):
        return (rep, value * N_Z + z)

    def at_z(value):
        return (rep, y * N_Z + value)

    def remote(src, dst, send, recv, device):
        return pltpu.make_async_remote_copy(
            src_ref=src, dst_ref=dst, send_sem=send, recv_sem=recv, device_id=device, device_id_type=MESH
        )

    target = (lax.rem(rep + offset, 32), fs)
    source = (lax.rem(rep + 32 - offset, 32), fs)
    slots = []
    if offset == 8:
        z_all = zh * N_Z + z
        z_down = lax.rem(z_all + 10, 16)
        z_up = lax.rem(z_all + 6, 16)
        down = (lax.div(z_down, N_Z) * 8 + xc, y * N_Z + lax.rem(z_down, N_Z))
        up = (lax.div(z_up, N_Z) * 8 + xc, y * N_Z + lax.rem(z_up, N_Z))
    else:
        next_zh = lax.rem(zh + 1, 4)
        prev_zh = lax.rem(zh + 3, 4)
        for sx, sc in CROSSING[offset]:
            dx = ((sx * 2 + (sc or 0) + offset) % 8) // 2
            if sc is None:
                dc = core
                is_src = x == sx
                is_relay = x != sx
                is_dst = x == dx
                src_rep = zh * 8 + sx * 2 + core
            else:
                dc = 1 - sc
                is_src = jnp.logical_and(x == sx, core == sc)
                is_relay = jnp.logical_and(x != sx, core == dc)
                is_dst = jnp.logical_and(x == dx, core == dc)
                src_rep = zh * 8 + sx * 2 + sc
            slots.append(
                dict(
                    sx=sx,
                    is_src=is_src,
                    is_relay=is_relay,
                    is_dst=is_dst,
                    src=(src_rep, fs),
                    dst=(next_zh * 8 + dx * 2 + dc, fs),
                    relay=[(zh * 8 + q * 2 + dc, fs) for q in range(4)],
                    back=[(prev_zh * 8 + q * 2 + dc, fs) for q in range(4)],
                )
            )

    barrier = pltpu.get_barrier_semaphore()

    def greet(device):
        pl.semaphore_signal(barrier, inc=1, device_id=device, device_id_type=MESH)

    for d in (1, 2, 3):
        greet(at_y(xor(y, d)))
        greet(at_z(xor(z, d)))
    greet(source)
    expected = 7
    if offset == 8:
        greet(up)
        expected = 8
    for slot in slots:

        @pl.when(slot["is_relay"])
        def _():
            greet(slot["src"])

        @pl.when(slot["is_dst"])
        def _():
            for q in range(4):
                if q != slot["sx"]:
                    greet(slot["back"][q])

        expected = expected + slot["is_relay"].astype(jnp.int32) + 3 * slot["is_src"].astype(jnp.int32)

    w_low[...] = w_ref[...].astype(BF16)
    pl.semaphore_wait(barrier, expected)

    def own_columns(peer, start, width):
        return pl.ds(pl.multiple_of(peer * SLICE + start, 128), width)

    w_copies, acts_copies = [], []
    cot_copies = [[] for _ in range(CHUNKS)]
    for d in (1, 2, 3):
        peer = xor(y, d)
        w_copies.append(
            remote(
                w_low.at[:, own_columns(peer, 0, SLICE)], w_full.at[y, z], s_w.at[d - 1], r_w.at[d - 1], at_y(peer)
            )
        )
        acts_copies.append(
            remote(acts_ref, acts_in.at[d - 1], s_acts.at[d - 1], r_acts.at[d - 1], at_y(peer))
        )
        for c in range(CHUNKS):
            cot_copies[c].append(
                remote(
                    cot_ref.at[:, own_columns(peer, c * CW, CW)],
                    cot_in.at[c, d],
                    s_cot.at[c, d - 1],
                    r_cot.at[c, d - 1],
                    at_y(peer),
                )
            )
    for copy in w_copies + acts_copies + cot_copies[0]:
        copy.start()
    w_full[y, z] = w_low[:, own_columns(y, 0, SLICE)]
    for c in range(1, CHUNKS):
        for copy in cot_copies[c]:
            copy.start()
    acts_t[0] = acts_ref[...].T
    for c in range(CHUNKS):
        cot_in[c, 0] = cot_ref[:, own_columns(y, c * CW, CW)]

    left = at_z(lax.rem(z + 3, 4))
    right = at_z(lax.rem(z + 1, 4))

    def pass_right(step):
        block = w_full.at[:, lax.rem(z + 4 - step, 4)]
        return remote(block, block, s_gz.at[0, step], r_gz.at[0, step], right)

    def pass_left(step):
        block = w_full.at[:, lax.rem(z + step, 4)]
        return remote(block, block, s_gz.at[1, step], r_gz.at[1, step], left)

    def gather_step(step):
        if step > 0:

            @pl.when(z >= step)
            def _():
                pass_right(step - 1).wait_recv()

            @pl.when(z <= 3 - step)
            def _():
                pass_left(step - 1).wait_recv()

        if step < 3:

            @pl.when(jnp.logical_and(z >= step, z < 3))
            def _():
                pass_right(step).start()

            @pl.when(jnp.logical_and(z <= 3 - step, z > 0))
            def _():
                pass_left(step).start()

    for copy in w_copies:
        copy.wait_recv()
    gather_step(0)

    for d in (1, 2, 3):
        acts_copies[d - 1].wait_recv()
        acts_t[d] = acts_in[d - 1].T
    gather_step(1)
    gather_step(2)

    rs_copies = [
        [
            remote(
                g_send.at[c, :, xor(z, d)], rs_in.at[c, d - 1], s_rs.at[c, d - 1], r_rs.at[c, d - 1], at_z(xor(z, d))
            )
            for d in (1, 2, 3)
        ]
        for c in range(CHUNKS)
    ]

    def gradient_chunk(c):
        for copy in cot_copies[c]:
            copy.wait_recv()
        for part in range(N_Y):
            total = None
            for d in range(4):
                term = jnp.dot(
                    acts_t[d, pl.ds(part * 128, 128), :], cot_in[c, d], preferred_element_type=F32
                )
                total = term if total is None else total + term
            g_send[c, part] = (OUT_SCALE * total).astype(BF16).reshape(N_Z, OWN, CW)
        for copy in rs_copies[c]:
            copy.start()

    gb_copies = [
        [
            remote(gb_send.at[c, xor(y, d)], gb_in.at[c, y], s_gb.at[c, d - 1], r_gb.at[c, d - 1], at_y(xor(y, d)))
            for d in (1, 2, 3)
        ]
        for c in range(CHUNKS)
    ]

    def reduce_chunk(c):
        for copy in rs_copies[c]:
            copy.wait_recv()
        total = g_send[c, :, z].astype(F32)
        for d in (1, 2, 3):
            total = total + rs_in[c, d - 1].astype(F32)
        gb_send[c] = total.astype(BF16)
        for copy in gb_copies[c]:
            copy.start()
        gb_in[c, y] = gb_send[c, y]

    learn = par_ref[0]
    scale_one = par_ref[1]
    scale_two = par_ref[2]

    def direct(c, q):
        return remote(go_send.at[c, q], go_in.at[c, q], s_go.at[c, q], r_go.at[c, q], target)

    def to_relay(c, q, slot_at, device):
        return remote(
            go_send.at[c, q], relay_in.at[c, slot_at], s_go.at[c, q], r_rel.at[c, slot_at], device
        )

    def go_on(c, q, slot_at, device):
        return remote(
            relay_in.at[c, slot_at], go_in.at[c, q], s_fwd.at[c, slot_at], r_go.at[c, q], device
        )

    def update_chunk(c):
        for copy in gb_copies[c]:
            copy.wait_recv()
        for q in range(4):
            columns = pl.ds(q * SLICE + c * CW, CW)
            grad = gb_in[c, q].astype(F32)
            weight = w_ref[:, columns]
            a_up = BETA_ONE * ma_ref[:, columns] + (1.0 - BETA_ONE) * grad
            b_up = BETA_TWO * mb_ref[:, columns] + (1.0 - BETA_TWO) * grad * grad
            direction = a_up * scale_one / (jnp.sqrt(b_up * scale_two) + EPSILON) + DECAY * weight
            w_up = weight - learn * direction
            go_send[c, q, 0] = w_up.astype(BF16)
            go_send[c, q, 1] = a_up.astype(BF16)
            go_send[c, q, 2] = b_up.astype(BF16)
            w_out[:, columns] = 0.5 * w_up
            ma_out[:, columns] = 0.5 * a_up
            mb_out[:, columns] = 0.5 * b_up
            if offset == 8:
                if q < 3:
                    direct(c, q).start()
                else:
                    to_relay(c, q, 0, down).start()
            else:
                by_relay = None
                for slot_at, slot in enumerate(slots):
                    if q != slot["sx"]:

                        @pl.when(slot["is_src"])
                        def _():
                            to_relay(c, q, slot_at, slot["relay"][q]).start()

                        by_relay = (
                            slot["is_src"] if by_relay is None else jnp.logical_or(by_relay, slot["is_src"])
                        )
                if by_relay is None:
                    direct(c, q).start()
                else:

                    @pl.when(jnp.logical_not(by_relay))
                    def _():
                        direct(c, q).start()

    def relay_chunk(c):
        if offset == 8:
            to_relay(c, 3, 0, down).wait_recv()
            go_on(c, 3, 0, down).start()
        for slot_at, slot in enumerate(slots):

            @pl.when(slot["is_relay"])
            def _():
                to_relay(c, 0, slot_at, target).wait_recv()
                go_on(c, x, slot_at, slot["dst"]).start()

    def mix_chunk(c):
        for q in range(4):
            direct(c, q).wait_recv()
            columns = pl.ds(q * SLICE + c * CW, CW)
            w_out[:, columns] += 0.5 * go_in[c, q, 0].astype(F32)
            ma_out[:, columns] += 0.5 * go_in[c, q, 1].astype(F32)
            mb_out[:, columns] += 0.5 * go_in[c, q, 2].astype(F32)

    def product(d):
        total = None
        for c in range(CHUNKS):
            block = w_full[:, :, :, pl.ds(c * CW, CW)].reshape(ROWS, CW)
            term = lax.dot_general(
                cot_in[c, d], block, (((1,), (1,)), ((), ())), preferred_element_type=F32
            )
            total = term if total is None else total + term
        return total

    ag_copies = [
        remote(ag_send.at[d - 1], ag_in.at[d - 1], s_ag.at[d - 1], r_ag.at[d - 1], at_y(xor(y, d)))
        for d in (1, 2, 3)
    ]

    def act_grad_send():
        gather_step(3)
        for d in (2, 1, 3):
            ag_send[d - 1] = product(d).astype(BF16)
            ag_copies[d - 1].start()

    def act_grad_end():
        total = product(0)
        for d in (1, 2, 3):
            ag_copies[d - 1].wait_recv()
            total = total + ag_in[d - 1].astype(F32)
        ag_out[...] = (OUT_SCALE * total).astype(BF16)

    gradient_chunk(0)
    gradient_chunk(1)
    reduce_chunk(0)
    gradient_chunk(2)
    reduce_chunk(1)
    update_chunk(0)
    gradient_chunk(3)
    act_grad_send()
    reduce_chunk(2)
    update_chunk(1)
    relay_chunk(0)
    reduce_chunk(3)
    update_chunk(2)
    relay_chunk(1)
    update_chunk(3)
    relay_chunk(2)
    relay_chunk(3)
    mix_chunk(0)
    mix_chunk(1)
    act_grad_end()
    mix_chunk(2)
    mix_chunk(3)

    for copies in [w_copies, acts_copies, ag_copies] + cot_copies + rs_copies + gb_copies:
        for copy in copies:
            copy.wait_send()
    for step in range(3):

        @pl.when(jnp.logical_and(z >= step, z < 3))
        def _():
            pass_right(step).wait_send()

        @pl.when(jnp.logical_and(z <= 3 - step, z > 0))
        def _():
            pass_left(step).wait_send()

    for c in range(CHUNKS):
        for q in range(4):
            direct(c, q).wait_send()
        if offset == 8:
            go_on(c, 3, 0, down).wait_send()
        for slot_at, slot in enumerate(slots):

            @pl.when(slot["is_relay"])
            def _():
                go_on(c, 0, slot_at, slot["dst"]).wait_send()


def step_kernel(offset, collective):
    n_slots = len(CROSSING.get(offset, ((0, None),)))
    dma = pltpu.SemaphoreType.DMA
    vmem = pl.BlockSpec(memory_space=pltpu.VMEM)
    return pl.pallas_call(
        partial(gossip_kernel, offset),
        out_shape=(
            jax.ShapeDtypeStruct((TOK, ROWS), BF16),
            jax.ShapeDtypeStruct((OWN, D), F32),
            jax.ShapeDtypeStruct((OWN, D), F32),
            jax.ShapeDtypeStruct((OWN, D), F32),
        ),
        in_specs=[pl.BlockSpec(memory_space=pltpu.SMEM)] + [vmem] * 5,
        out_specs=(vmem,) * 4,
        scratch_shapes=[
            pltpu.VMEM((OWN, D), BF16),
            pltpu.VMEM((N_Y, N_Z, OWN, SLICE), BF16),
            pltpu.VMEM((3, TOK, ROWS), BF16),
            pltpu.VMEM((4, ROWS, TOK), BF16),
            pltpu.VMEM((CHUNKS, 4, TOK, CW), BF16),
            pltpu.VMEM((CHUNKS, N_Y, N_Z, OWN, CW), BF16),
            pltpu.VMEM((CHUNKS, 3, N_Y, OWN, CW), BF16),
            pltpu.VMEM((CHUNKS, N_Y, OWN, CW), BF16),
            pltpu.VMEM((CHUNKS, N_Y, OWN, CW), BF16),
            pltpu.VMEM((3, TOK, ROWS), BF16),
            pltpu.VMEM((3, TOK, ROWS), BF16),
            pltpu.VMEM((CHUNKS, 4, 3, OWN, CW), BF16),
            pltpu.VMEM((CHUNKS, 4, 3, OWN, CW), BF16),
            pltpu.VMEM((CHUNKS, n_slots, 3, OWN, CW), BF16),
            dma((3,)),
            dma((3,)),
            dma((3,)),
            dma((3,)),
            dma((CHUNKS, 3)),
            dma((CHUNKS, 3)),
            dma((2, 3)),
            dma((2, 3)),
            dma((CHUNKS, 3)),
            dma((CHUNKS, 3)),
            dma((CHUNKS, 3)),
            dma((CHUNKS, 3)),
            dma((3,)),
            dma((3,)),
            dma((CHUNKS, 4)),
            dma((CHUNKS, 4)),
            dma((CHUNKS, n_slots)),
            dma((CHUNKS, n_slots)),
            dma((CHUNKS, n_slots)),
        ],
        compiler_params=pltpu.CompilerParams(
            collective_id=collective, has_side_effects=True, vmem_limit_bytes=48 << 20
        ),
        name="gossip_step_%d" % offset,
    )


def local(acts, cotangent, weight, moment_one, moment_two, learn_rate, step_index, step_count):
    steps_float = step_count[0].astype(F32)
    fix_one = 1.0 - jnp.power(F32(BETA_ONE), steps_float)
    fix_two = 1.0 - jnp.power(F32(BETA_TWO), steps_float)
    numbers = jnp.stack([learn_rate[0], 1.0 / fix_one, 1.0 / fix_two])
    outs = lax.switch(
        step_index[0] % 4,
        [step_kernel(1 << level, level) for level in range(4)],
        numbers,
        acts[0],
        cotangent[0],
        weight[0],
        moment_one[0],
        moment_two[0],
    )
    return tuple(out[None] for out in outs)


def solution(mesh):
    split = P("rep", "fsdp", None)
    return jax.shard_map(
        local,
        mesh=mesh,
        in_specs=(split,) * 5 + (P(),) * 3,
        out_specs=(split,) * 4,
        check_vma=False,
    )
```

```python
from functools import partial

import jax
import jax.numpy as jnp
from jax import lax
from jax.experimental import pallas as pl
from jax.experimental.pallas import tpu as pltpu
from jax.sharding import PartitionSpec as P

BETA_ONE = 0.9
BETA_TWO = 0.95
EPSILON = 1e-08
DECAY = 0.1
OUT_SCALE = 0.015625

MESH = pl.DeviceIdType.MESH
F32 = jnp.float32
BF16 = jnp.bfloat16

N_Y = 4
N_Z = 4
TOK = 192
ROWS = 512
OWN = 32
D = 4096
SLICE = D // N_Y
CHUNKS = 4
CW = SLICE // CHUNKS
HALF = SLICE // 2

STRAIGHT = 1
EARLY = {1: 1, 2: 1, 4: 1, 8: 1}

CROSSING = {1: ((3, 1),), 2: ((3, None),), 4: ((2, None), (3, None))}


def xor(index, bits):
    low = lax.rem(index, 2)
    high = lax.div(index, 2)
    if bits & 1:
        low = 1 - low
    if bits & 2:
        high = 1 - high
    return high * 2 + low


def gossip_kernel(
    offset,
    par_ref,
    acts_ref,
    cot_ref,
    w_hbm,
    ma_hbm,
    mb_hbm,
    ag_out,
    w_out,
    ma_out,
    mb_out,
    w_ref,
    ma_ref,
    mb_ref,
    w_low,
    w_full,
    acts_in,
    acts_t,
    cot_in,
    g_send,
    rs_in,
    total,
    gb_send,
    gb_in,
    ag_send,
    ag_in,
    ag_sum,
    go_send,
    go_in,
    relay_in,
    gg_in,
    relay_gg,
    s_w,
    r_w,
    s_acts,
    r_acts,
    s_cot,
    r_cot,
    s_gz,
    r_gz,
    s_rs,
    r_rs,
    s_gb,
    r_gb,
    s_ag,
    r_ag,
    s_go,
    r_go,
    r_rel,
    s_fwd,
    s_gg,
    r_gg,
    r_relg,
    s_fwdg,
    s_own,
):
    rep = lax.axis_index("rep")
    fs = lax.axis_index("fsdp")
    zh = lax.div(rep, 8)
    xc = lax.rem(rep, 8)
    x = lax.div(xc, 2)
    core = lax.rem(rep, 2)
    y = lax.div(fs, N_Z)
    z = lax.rem(fs, N_Z)

    def at_y(value):
        return (rep, value * N_Z + z)

    def at_z(value):
        return (rep, y * N_Z + value)

    def remote(src, dst, send, recv, device):
        return pltpu.make_async_remote_copy(
            src_ref=src, dst_ref=dst, send_sem=send, recv_sem=recv, device_id=device, device_id_type=MESH
        )

    target = (lax.rem(rep + offset, 32), fs)
    source = (lax.rem(rep + 32 - offset, 32), fs)
    slots = []
    if offset == 8:
        z_all = zh * N_Z + z
        z_down = lax.rem(z_all + 10, 16)
        z_up = lax.rem(z_all + 6, 16)
        down = (lax.div(z_down, N_Z) * 8 + xc, y * N_Z + lax.rem(z_down, N_Z))
        up = (lax.div(z_up, N_Z) * 8 + xc, y * N_Z + lax.rem(z_up, N_Z))
    else:
        next_zh = lax.rem(zh + 1, 4)
        prev_zh = lax.rem(zh + 3, 4)
        for sx, sc in CROSSING[offset]:
            dx = ((sx * 2 + (sc or 0) + offset) % 8) // 2
            if sc is None:
                dc = core
                is_src = x == sx
                is_relay = x != sx
                is_dst = x == dx
                src_rep = zh * 8 + sx * 2 + core
            else:
                dc = 1 - sc
                is_src = jnp.logical_and(x == sx, core == sc)
                is_relay = jnp.logical_and(x != sx, core == dc)
                is_dst = jnp.logical_and(x == dx, core == dc)
                src_rep = zh * 8 + sx * 2 + sc
            slots.append(
                dict(
                    sx=sx,
                    is_src=is_src,
                    is_relay=is_relay,
                    is_dst=is_dst,
                    src=(src_rep, fs),
                    dst=(next_zh * 8 + dx * 2 + dc, fs),
                    relay=[(zh * 8 + q * 2 + dc, fs) for q in range(4)],
                    back=[(prev_zh * 8 + q * 2 + dc, fs) for q in range(4)],
                )
            )

    barrier = pltpu.get_barrier_semaphore()

    def greet(device):
        pl.semaphore_signal(barrier, inc=1, device_id=device, device_id_type=MESH)

    for d in (1, 2, 3):
        greet(at_y(xor(y, d)))
    for d in (1, 2, 3):
        greet(at_z(xor(z, d)))
    greet(source)
    expected = 7
    if offset == 8:
        greet(up)
        expected = 8
    for slot in slots:

        @pl.when(slot["is_relay"])
        def _():
            greet(slot["src"])

        @pl.when(slot["is_dst"])
        def _():
            for q in range(4):
                if q != slot["sx"]:
                    greet(slot["back"][q])

        expected = expected + slot["is_relay"].astype(jnp.int32) + 3 * slot["is_src"].astype(jnp.int32)

    early = EARLY[offset]
    first_early = CHUNKS - early
    first_straight = CHUNKS - STRAIGHT

    def part(q, c):
        return pl.ds(q * SLICE + c * CW, CW)

    def chunk(c):
        return pl.ds(c * CW, CW)

    def tokens(d):
        return pl.ds(d * TOK, TOK)

    own_cot = cot_ref.at[:, pl.ds(pl.multiple_of(y * SLICE, 128), SLICE)]
    own_copies = [
        pltpu.make_async_copy(src, dst, s_own.at[i])
        for i, (src, dst) in enumerate(
            (
                (w_hbm, w_ref),
                (acts_ref, acts_in.at[tokens(0)]),
                (own_cot, cot_in.at[tokens(0)]),
                (ma_hbm, ma_ref),
                (mb_hbm, mb_ref),
            )
        )
    ]
    for copy in own_copies:
        copy.start()
    own_copies[0].wait()
    w_low[...] = w_ref[...].astype(BF16)
    pl.semaphore_wait(barrier, expected)

    def own_columns(peer, start, width):
        return pl.ds(pl.multiple_of(peer * SLICE + start, 128), width)

    w_copies, acts_copies = [[], []], []
    cot_copies = [[] for _ in range(CHUNKS)]
    for d in (1, 2, 3):
        peer = xor(y, d)
        for h in range(2):
            w_copies[h].append(
                remote(
                    w_low.at[:, own_columns(peer, h * HALF, HALF)],
                    w_full.at[h, y, z],
                    s_w.at[h, d - 1],
                    r_w.at[h, d - 1],
                    at_y(peer),
                )
            )
        acts_copies.append(
            remote(acts_ref, acts_in.at[tokens(d)], s_acts.at[d - 1], r_acts.at[d - 1], at_y(peer))
        )
        for c in range(CHUNKS):
            cot_copies[c].append(
                remote(
                    cot_ref.at[:, own_columns(peer, c * CW, CW)],
                    cot_in.at[tokens(d), chunk(c)],
                    s_cot.at[c, d - 1],
                    r_cot.at[c, d - 1],
                    at_y(peer),
                )
            )
    for copy in w_copies[0] + w_copies[1] + acts_copies:
        copy.start()
    for c in range(CHUNKS):
        for copy in cot_copies[c]:
            copy.start()

    def ends(kind, c, q):
        if kind == 0:
            return go_send.at[c, q], go_in.at[c, q], s_go.at[c, q], r_go.at[c, q]
        e = c - first_early
        return gb_in.at[c, q], gg_in.at[e, q], s_gg.at[e, q], r_gg.at[e, q]

    def middle(kind, c, slot_at):
        if kind == 0:
            return relay_in.at[c, slot_at], r_rel.at[c, slot_at], s_fwd.at[c, slot_at]
        e = c - first_early
        return relay_gg.at[e, slot_at], r_relg.at[e, slot_at], s_fwdg.at[e, slot_at]

    def direct(kind, c, q):
        src, dst, send, recv = ends(kind, c, q)
        return remote(src, dst, send, recv, target)

    def to_relay(kind, c, q, slot_at, device):
        src, _, send, _ = ends(kind, c, q)
        hold, recv, _ = middle(kind, c, slot_at)
        return remote(src, hold, send, recv, device)

    def go_on(kind, c, q, slot_at, device):
        _, dst, _, recv = ends(kind, c, q)
        hold, _, send = middle(kind, c, slot_at)
        return remote(hold, dst, send, recv, device)

    def gossip_send(kind, c, q):
        if offset == 8:
            if q < 3:
                direct(kind, c, q).start()
            else:
                to_relay(kind, c, q, 0, down).start()
            return
        by_relay = None
        for slot_at, slot in enumerate(slots):
            if q != slot["sx"]:

                @pl.when(slot["is_src"])
                def _():
                    to_relay(kind, c, q, slot_at, slot["relay"][q]).start()

                by_relay = slot["is_src"] if by_relay is None else jnp.logical_or(by_relay, slot["is_src"])
        if by_relay is None:
            direct(kind, c, q).start()
        else:

            @pl.when(jnp.logical_not(by_relay))
            def _():
                direct(kind, c, q).start()

    def relay_chunk(kind, c):
        if offset == 8:
            to_relay(kind, c, 3, 0, down).wait_recv()
            go_on(kind, c, 3, 0, down).start()
        for slot_at, slot in enumerate(slots):

            @pl.when(slot["is_relay"])
            def _():
                to_relay(kind, c, 0, slot_at, target).wait_recv()
                go_on(kind, c, x, slot_at, slot["dst"]).start()

    def gossip_end(kind, c):
        for q in range(4):
            direct(kind, c, q).wait_send()
        if offset == 8:
            go_on(kind, c, 3, 0, down).wait_send()
        for slot_at, slot in enumerate(slots):

            @pl.when(slot["is_relay"])
            def _():
                go_on(kind, c, 0, slot_at, slot["dst"]).wait_send()

    for h in range(2):
        w_full[h, y, z] = w_low[:, own_columns(y, h * HALF, HALF)]
    for copy in own_copies[1:]:
        copy.wait()
    for c in range(first_early, CHUNKS):
        for q in range(4):
            go_send[c, q, 0] = w_low[:, part(q, c)]
            go_send[c, q, 1] = ma_ref[:, part(q, c)].astype(BF16)
            go_send[c, q, 2] = mb_ref[:, part(q, c)].astype(BF16)
            gossip_send(0, c, q)

    left = at_z(lax.rem(z + 3, 4))
    right = at_z(lax.rem(z + 1, 4))

    def pass_right(h, step):
        block = w_full.at[h, :, lax.rem(z + 4 - step, 4)]
        return remote(block, block, s_gz.at[h, 0, step], r_gz.at[h, 0, step], right)

    def pass_left(h, step):
        block = w_full.at[h, :, lax.rem(z + step, 4)]
        return remote(block, block, s_gz.at[h, 1, step], r_gz.at[h, 1, step], left)

    def gather_step(h, step):
        if step == 0:
            for copy in w_copies[h]:
                copy.wait_recv()
        else:

            @pl.when(z >= step)
            def _():
                pass_right(h, step - 1).wait_recv()

            @pl.when(z <= 3 - step)
            def _():
                pass_left(h, step - 1).wait_recv()

        if step < 3:

            @pl.when(jnp.logical_and(z >= step, z < 3))
            def _():
                pass_right(h, step).start()

            @pl.when(jnp.logical_and(z <= 3 - step, z > 0))
            def _():
                pass_left(h, step).start()

    def activations():
        for copy in acts_copies:
            copy.wait_recv()
        acts_t[...] = acts_in[...].T

    def sum_right(c, t):
        return remote(g_send.at[c, :, t], rs_in.at[0, c, t], s_rs.at[0, c, t], r_rs.at[0, c, t], right)

    def sum_left(c, t):
        return remote(g_send.at[c, :, t], rs_in.at[1, c, t], s_rs.at[1, c, t], r_rs.at[1, c, t], left)

    def straight(c, d):
        peer = xor(z, d)
        return remote(g_send.at[c, :, peer], rs_in.at[0, c, d], s_rs.at[0, c, d], r_rs.at[0, c, d], at_z(peer))

    def add_and_pass(c, t, way):
        copy = (sum_right, sum_left)[way](c, t)
        copy.wait_recv()
        g_send[c, :, t] = (g_send[c, :, t].astype(F32) + rs_in[way, c, t].astype(F32)).astype(BF16)
        copy.start()

    def pass_one(c):
        @pl.when(z == 1)
        def _():
            add_and_pass(c, 3, 0)
            add_and_pass(c, 2, 0)

        @pl.when(z == 2)
        def _():
            add_and_pass(c, 0, 1)
            add_and_pass(c, 1, 1)

    def pass_two(c):
        @pl.when(z == 2)
        def _():
            add_and_pass(c, 3, 0)

        @pl.when(z == 1)
        def _():
            add_and_pass(c, 0, 1)

    def gradient_chunk(c):
        for copy in cot_copies[c]:
            copy.wait_recv()
        result = jnp.dot(acts_t[...], cot_in[:, chunk(c)], preferred_element_type=F32)
        g_send[c] = (OUT_SCALE * result).astype(BF16).reshape(N_Y, N_Z, OWN, CW)
        if c >= first_straight:
            for d in (2, 3, 1):
                straight(c, d).start()
        else:

            @pl.when(z == 0)
            def _():
                for t in (3, 2, 1):
                    sum_right(c, t).start()

            @pl.when(z == 3)
            def _():
                for t in (0, 1, 2):
                    sum_left(c, t).start()

    gb_copies = [
        [
            remote(gb_send.at[c, xor(y, d)], gb_in.at[c, y], s_gb.at[c, d - 1], r_gb.at[c, d - 1], at_y(xor(y, d)))
            for d in (1, 2, 3)
        ]
        for c in range(CHUNKS)
    ]

    def reduce_chunk(c):
        if c >= first_straight:
            result = g_send[c, :, z].astype(F32)
            for d in (1, 2, 3):
                straight(c, d).wait_recv()
                result = result + rs_in[0, c, d].astype(F32)
            gb_send[c] = result.astype(BF16)
        else:
            total[...] = g_send[c, :, z].astype(F32)

            @pl.when(z > 0)
            def _():
                sum_right(c, z).wait_recv()
                total[...] += rs_in[0, c, z].astype(F32)

            @pl.when(z < 3)
            def _():
                sum_left(c, z).wait_recv()
                total[...] += rs_in[1, c, z].astype(F32)

            gb_send[c] = total[...].astype(BF16)
        for copy in gb_copies[c]:
            copy.start()
        gb_in[c, y] = gb_send[c, y]

    learn = par_ref[0]
    scale_one = par_ref[1]
    scale_two = par_ref[2]

    def adamw(weight, moment_a, moment_b, grad):
        a_up = BETA_ONE * moment_a + (1.0 - BETA_ONE) * grad
        b_up = BETA_TWO * moment_b + (1.0 - BETA_TWO) * grad * grad
        direction = a_up * scale_one / (jnp.sqrt(b_up * scale_two) + EPSILON) + DECAY * weight
        return weight - learn * direction, a_up, b_up

    def update_chunk(c):
        for copy in gb_copies[c]:
            copy.wait_recv()
        if c >= first_early:
            for q in range(4):
                gossip_send(1, c, q)
        for q in range(4):
            columns = part(q, c)
            w_up, a_up, b_up = adamw(
                w_ref[:, columns], ma_ref[:, columns], mb_ref[:, columns], gb_in[c, q].astype(F32)
            )
            if c < first_early:
                go_send[c, q, 0] = w_up.astype(BF16)
                go_send[c, q, 1] = a_up.astype(BF16)
                go_send[c, q, 2] = b_up.astype(BF16)
                gossip_send(0, c, q)
            w_out[:, columns] = 0.5 * w_up
            ma_out[:, columns] = 0.5 * a_up
            mb_out[:, columns] = 0.5 * b_up

    def mix_chunk(c):
        for q in range(4):
            direct(0, c, q).wait_recv()
            columns = part(q, c)
            w_up, a_up, b_up = (go_in[c, q, k].astype(F32) for k in range(3))
            if c >= first_early:
                direct(1, c, q).wait_recv()
                w_up, a_up, b_up = adamw(w_up, a_up, b_up, gg_in[c - first_early, q].astype(F32))
            w_out[:, columns] += 0.5 * w_up
            ma_out[:, columns] += 0.5 * a_up
            mb_out[:, columns] += 0.5 * b_up

    def product(d, h):
        return lax.dot_general(
            cot_in[tokens(d), pl.ds(h * HALF, HALF)],
            w_full[h].reshape(ROWS, HALF),
            (((1,), (1,)), ((), ())),
            preferred_element_type=F32,
        )

    def act_grad_start(d):
        ag_sum[d] = product(d, 0)

    ag_copies = [
        remote(ag_send.at[d - 1], ag_in.at[d - 1], s_ag.at[d - 1], r_ag.at[d - 1], at_y(xor(y, d)))
        for d in (1, 2, 3)
    ]

    def act_grad_send(d):
        ag_send[d - 1] = (ag_sum[d] + product(d, 1)).astype(BF16)
        ag_copies[d - 1].start()

    def act_grad_end():
        result = ag_sum[0] + product(0, 1)
        for d in (1, 2, 3):
            ag_copies[d - 1].wait_recv()
            result = result + ag_in[d - 1].astype(F32)
        ag_out[...] = (OUT_SCALE * result).astype(BF16)

    steps = [
        (8.0, gather_step, 0, 0),
        (9.5, gather_step, 1, 0),
        (12.5, gather_step, 0, 1),
        (15.5, gather_step, 1, 1),
        (16.0, activations),
        (17.5, gather_step, 0, 2),
        (20.5, gather_step, 1, 2),
        (22.0, gather_step, 0, 3),
        (26.5, gather_step, 1, 3),
        (23.5, act_grad_start, 0),
        (24.0, act_grad_start, 2),
        (25.0, act_grad_start, 1),
        (26.0, act_grad_start, 3),
        (29.3, act_grad_send, 2),
        (30.0, act_grad_send, 1),
        (30.7, act_grad_send, 3),
        (42.0, act_grad_end),
    ]
    for c in range(CHUNKS):
        at = 17.0 + 12.0 / CHUNKS * (c + 1)
        steps.append((at, gradient_chunk, c))
        if c >= first_straight:
            at += 5.0
        else:
            steps.append((at + 3.0, pass_one, c))
            steps.append((at + 5.5, pass_two, c))
            at += 8.0
        steps.append((at, reduce_chunk, c))
        at += 2.5
        steps.append((at, update_chunk, c))
        if c >= first_early:
            steps.append((16.2, relay_chunk, 0, c))
            steps.append((at + 3.0, relay_chunk, 1, c))
        else:
            steps.append((at + 4.0, relay_chunk, 0, c))
        steps.append((at + 8.0, mix_chunk, c))
    for _, act, *with_args in sorted(steps, key=lambda step: step[0]):
        act(*with_args)

    for copies in w_copies + [acts_copies, ag_copies] + cot_copies + gb_copies:
        for copy in copies:
            copy.wait_send()
    for h in range(2):
        for step in range(3):

            @pl.when(jnp.logical_and(z >= step, z < 3))
            def _():
                pass_right(h, step).wait_send()

            @pl.when(jnp.logical_and(z <= 3 - step, z > 0))
            def _():
                pass_left(h, step).wait_send()

    for c in range(CHUNKS):
        if c >= first_straight:
            for d in (1, 2, 3):
                straight(c, d).wait_send()
        else:
            for t in range(N_Z):

                @pl.when(z < t)
                def _():
                    sum_right(c, t).wait_send()

                @pl.when(z > t)
                def _():
                    sum_left(c, t).wait_send()

        gossip_end(0, c)
        if c >= first_early:
            gossip_end(1, c)


def step_kernel(offset, collective):
    n_slots = len(CROSSING.get(offset, ((0, None),)))
    early = max(EARLY[offset], 1)
    dma = pltpu.SemaphoreType.DMA
    vmem = pl.BlockSpec(memory_space=pltpu.VMEM)
    return pl.pallas_call(
        partial(gossip_kernel, offset),
        out_shape=(
            jax.ShapeDtypeStruct((TOK, ROWS), BF16),
            jax.ShapeDtypeStruct((OWN, D), F32),
            jax.ShapeDtypeStruct((OWN, D), F32),
            jax.ShapeDtypeStruct((OWN, D), F32),
        ),
        in_specs=[pl.BlockSpec(memory_space=pltpu.SMEM)] + [pl.BlockSpec(memory_space=pltpu.HBM)] * 5,
        out_specs=(vmem,) * 4,
        scratch_shapes=[pltpu.VMEM((OWN, D), F32)] * 3
        + [
            pltpu.VMEM((OWN, D), BF16),
            pltpu.VMEM((2, N_Y, N_Z, OWN, HALF), BF16),
            pltpu.VMEM((4 * TOK, ROWS), BF16),
            pltpu.VMEM((ROWS, 4 * TOK), BF16),
            pltpu.VMEM((4 * TOK, SLICE), BF16),
            pltpu.VMEM((CHUNKS, N_Y, N_Z, OWN, CW), BF16),
            pltpu.VMEM((2, CHUNKS, N_Z, N_Y, OWN, CW), BF16),
            pltpu.VMEM((N_Y, OWN, CW), F32),
            pltpu.VMEM((CHUNKS, N_Y, OWN, CW), BF16),
            pltpu.VMEM((CHUNKS, N_Y, OWN, CW), BF16),
            pltpu.VMEM((3, TOK, ROWS), BF16),
            pltpu.VMEM((3, TOK, ROWS), BF16),
            pltpu.VMEM((4, TOK, ROWS), F32),
            pltpu.VMEM((CHUNKS, 4, 3, OWN, CW), BF16),
            pltpu.VMEM((CHUNKS, 4, 3, OWN, CW), BF16),
            pltpu.VMEM((CHUNKS, n_slots, 3, OWN, CW), BF16),
            pltpu.VMEM((early, 4, OWN, CW), BF16),
            pltpu.VMEM((early, n_slots, OWN, CW), BF16),
            dma((2, 3)),
            dma((2, 3)),
            dma((3,)),
            dma((3,)),
            dma((CHUNKS, 3)),
            dma((CHUNKS, 3)),
            dma((2, 2, 3)),
            dma((2, 2, 3)),
            dma((2, CHUNKS, N_Z)),
            dma((2, CHUNKS, N_Z)),
            dma((CHUNKS, 3)),
            dma((CHUNKS, 3)),
            dma((3,)),
            dma((3,)),
            dma((CHUNKS, 4)),
            dma((CHUNKS, 4)),
            dma((CHUNKS, n_slots)),
            dma((CHUNKS, n_slots)),
            dma((early, 4)),
            dma((early, 4)),
            dma((early, n_slots)),
            dma((early, n_slots)),
            dma((5,)),
        ],
        compiler_params=pltpu.CompilerParams(
            collective_id=collective, has_side_effects=True, vmem_limit_bytes=58 << 20
        ),
        name="gossip_step_%d" % offset,
    )


def local(acts, cotangent, weight, moment_one, moment_two, learn_rate, step_index, step_count):
    steps_float = step_count[0].astype(F32)
    fix_one = 1.0 - jnp.power(F32(BETA_ONE), steps_float)
    fix_two = 1.0 - jnp.power(F32(BETA_TWO), steps_float)
    numbers = jnp.stack([learn_rate[0], 1.0 / fix_one, 1.0 / fix_two])
    outs = lax.switch(
        step_index[0] % 4,
        [step_kernel(1 << level, level) for level in range(4)],
        numbers,
        acts[0],
        cotangent[0],
        weight[0],
        moment_one[0],
        moment_two[0],
    )
    return tuple(out[None] for out in outs)


def solution(mesh):
    split = P("rep", "fsdp", None)
    return jax.shard_map(
        local,
        mesh=mesh,
        in_specs=(split,) * 5 + (P(),) * 3,
        out_specs=(split,) * 4,
        check_vma=False,
    )
```

```python
from functools import partial

import jax
import jax.numpy as jnp
from jax import lax
from jax.experimental import pallas as pl
from jax.experimental.pallas import tpu as pltpu
from jax.sharding import PartitionSpec as P

BETA_ONE = 0.9
BETA_TWO = 0.95
EPSILON = 1e-08
DECAY = 0.1
OUT_SCALE = 0.015625

MESH = pl.DeviceIdType.MESH
F32 = jnp.float32
BF16 = jnp.bfloat16

N_Y = 4
N_Z = 4
TOK = 192
ROWS = 512
OWN = 32
D = 4096
SLICE = D // N_Y
CHUNKS = 4
CW = SLICE // CHUNKS
HALF = SLICE // 2

STRAIGHT = 1
EARLY = {1: 1, 2: 1, 4: 1, 8: 1}

CROSSING = {1: ((3, 1),), 2: ((3, None),), 4: ((2, None), (3, None))}


def xor(index, bits):
    low = lax.rem(index, 2)
    high = lax.div(index, 2)
    if bits & 1:
        low = 1 - low
    if bits & 2:
        high = 1 - high
    return high * 2 + low


def gossip_kernel(
    offset,
    par_ref,
    acts_ref,
    cot_ref,
    w_hbm,
    ma_hbm,
    mb_hbm,
    ag_out,
    w_out,
    ma_out,
    mb_out,
    w_ref,
    ma_ref,
    mb_ref,
    w_low,
    w_full,
    acts_in,
    acts_t,
    cot_in,
    g_send,
    rs_in,
    total,
    gb_send,
    gb_in,
    ag_send,
    ag_in,
    ag_sum,
    go_send,
    go_in,
    relay_in,
    gg_in,
    relay_gg,
    s_w,
    r_w,
    s_acts,
    r_acts,
    s_cot,
    r_cot,
    s_gz,
    r_gz,
    s_rs,
    r_rs,
    s_gb,
    r_gb,
    s_ag,
    r_ag,
    s_go,
    r_go,
    r_rel,
    s_fwd,
    s_gg,
    r_gg,
    r_relg,
    s_fwdg,
    s_own,
):
    rep = lax.axis_index("rep")
    fs = lax.axis_index("fsdp")
    zh = lax.div(rep, 8)
    xc = lax.rem(rep, 8)
    x = lax.div(xc, 2)
    core = lax.rem(rep, 2)
    y = lax.div(fs, N_Z)
    z = lax.rem(fs, N_Z)

    def at_y(value):
        return (rep, value * N_Z + z)

    def at_z(value):
        return (rep, y * N_Z + value)

    def remote(src, dst, send, recv, device):
        return pltpu.make_async_remote_copy(
            src_ref=src, dst_ref=dst, send_sem=send, recv_sem=recv, device_id=device, device_id_type=MESH
        )

    target = (lax.rem(rep + offset, 32), fs)
    source = (lax.rem(rep + 32 - offset, 32), fs)
    slots = []
    if offset == 8:
        z_all = zh * N_Z + z
        z_down = lax.rem(z_all + 10, 16)
        z_up = lax.rem(z_all + 6, 16)
        down = (lax.div(z_down, N_Z) * 8 + xc, y * N_Z + lax.rem(z_down, N_Z))
        up = (lax.div(z_up, N_Z) * 8 + xc, y * N_Z + lax.rem(z_up, N_Z))
    else:
        next_zh = lax.rem(zh + 1, 4)
        prev_zh = lax.rem(zh + 3, 4)
        for sx, sc in CROSSING[offset]:
            dx = ((sx * 2 + (sc or 0) + offset) % 8) // 2
            if sc is None:
                dc = core
                is_src = x == sx
                is_relay = x != sx
                is_dst = x == dx
                src_rep = zh * 8 + sx * 2 + core
            else:
                dc = 1 - sc
                is_src = jnp.logical_and(x == sx, core == sc)
                is_relay = jnp.logical_and(x != sx, core == dc)
                is_dst = jnp.logical_and(x == dx, core == dc)
                src_rep = zh * 8 + sx * 2 + sc
            slots.append(
                dict(
                    sx=sx,
                    is_src=is_src,
                    is_relay=is_relay,
                    is_dst=is_dst,
                    src=(src_rep, fs),
                    dst=(next_zh * 8 + dx * 2 + dc, fs),
                    relay=[(zh * 8 + q * 2 + dc, fs) for q in range(4)],
                    back=[(prev_zh * 8 + q * 2 + dc, fs) for q in range(4)],
                )
            )

    barrier = pltpu.get_barrier_semaphore()

    def greet(device):
        pl.semaphore_signal(barrier, inc=1, device_id=device, device_id_type=MESH)

    for d in (1, 2, 3):
        greet(at_y(xor(y, d)))
    for d in (1, 2, 3):
        greet(at_z(xor(z, d)))
    greet(source)
    expected = 7
    if offset == 8:
        greet(up)
        expected = 8
    for slot in slots:

        @pl.when(slot["is_relay"])
        def _():
            greet(slot["src"])

        @pl.when(slot["is_dst"])
        def _():
            for q in range(4):
                if q != slot["sx"]:
                    greet(slot["back"][q])

        expected = expected + slot["is_relay"].astype(jnp.int32) + 3 * slot["is_src"].astype(jnp.int32)

    early = EARLY[offset]
    first_early = CHUNKS - early
    first_straight = CHUNKS - STRAIGHT

    def part(q, c):
        return pl.ds(q * SLICE + c * CW, CW)

    def chunk(c):
        return pl.ds(c * CW, CW)

    def tokens(d):
        return pl.ds(d * TOK, TOK)

    own_cot = cot_ref.at[:, pl.ds(pl.multiple_of(y * SLICE, 128), SLICE)]
    own_copies = [
        pltpu.make_async_copy(src, dst, s_own.at[i])
        for i, (src, dst) in enumerate(
            (
                (w_hbm, w_ref),
                (acts_ref, acts_in.at[tokens(0)]),
                (own_cot, cot_in.at[tokens(0)]),
                (ma_hbm, ma_ref),
                (mb_hbm, mb_ref),
            )
        )
    ]
    for copy in own_copies:
        copy.start()
    own_copies[0].wait()
    w_low[...] = w_ref[...].astype(BF16)
    pl.semaphore_wait(barrier, expected)

    def own_columns(peer, start, width):
        return pl.ds(pl.multiple_of(peer * SLICE + start, 128), width)

    w_copies, acts_copies = [[], []], []
    cot_copies = [[] for _ in range(CHUNKS)]
    for d in (1, 2, 3):
        peer = xor(y, d)
        for h in range(2):
            w_copies[h].append(
                remote(
                    w_low.at[:, own_columns(peer, h * HALF, HALF)],
                    w_full.at[h, y, z],
                    s_w.at[h, d - 1],
                    r_w.at[h, d - 1],
                    at_y(peer),
                )
            )
        acts_copies.append(
            remote(acts_ref, acts_in.at[tokens(d)], s_acts.at[d - 1], r_acts.at[d - 1], at_y(peer))
        )
        for c in range(CHUNKS):
            cot_copies[c].append(
                remote(
                    cot_ref.at[:, own_columns(peer, c * CW, CW)],
                    cot_in.at[tokens(d), chunk(c)],
                    s_cot.at[c, d - 1],
                    r_cot.at[c, d - 1],
                    at_y(peer),
                )
            )
    for copy in w_copies[0] + w_copies[1] + acts_copies:
        copy.start()
    for c in range(CHUNKS):
        for copy in cot_copies[c]:
            copy.start()

    def ends(kind, c, q):
        if kind == 0:
            return go_send.at[c, q], go_in.at[c, q], s_go.at[c, q], r_go.at[c, q]
        e = c - first_early
        return gb_in.at[c, q], gg_in.at[e, q], s_gg.at[e, q], r_gg.at[e, q]

    def middle(kind, c, slot_at):
        if kind == 0:
            return relay_in.at[c, slot_at], r_rel.at[c, slot_at], s_fwd.at[c, slot_at]
        e = c - first_early
        return relay_gg.at[e, slot_at], r_relg.at[e, slot_at], s_fwdg.at[e, slot_at]

    def direct(kind, c, q):
        src, dst, send, recv = ends(kind, c, q)
        return remote(src, dst, send, recv, target)

    def to_relay(kind, c, q, slot_at, device):
        src, _, send, _ = ends(kind, c, q)
        hold, recv, _ = middle(kind, c, slot_at)
        return remote(src, hold, send, recv, device)

    def go_on(kind, c, q, slot_at, device):
        _, dst, _, recv = ends(kind, c, q)
        hold, _, send = middle(kind, c, slot_at)
        return remote(hold, dst, send, recv, device)

    def gossip_send(kind, c, q):
        if kind == 1 and offset == 1:
            direct(kind, c, q).start()
            return
        if offset == 8:
            if q < 3:
                direct(kind, c, q).start()
            else:
                to_relay(kind, c, q, 0, down).start()
            return
        by_relay = None
        for slot_at, slot in enumerate(slots):
            if q != slot["sx"]:

                @pl.when(slot["is_src"])
                def _():
                    to_relay(kind, c, q, slot_at, slot["relay"][q]).start()

                by_relay = slot["is_src"] if by_relay is None else jnp.logical_or(by_relay, slot["is_src"])
        if by_relay is None:
            direct(kind, c, q).start()
        else:

            @pl.when(jnp.logical_not(by_relay))
            def _():
                direct(kind, c, q).start()

    def relay_chunk(kind, c):
        if kind == 1 and offset == 1:
            return
        if offset == 8:
            to_relay(kind, c, 3, 0, down).wait_recv()
            go_on(kind, c, 3, 0, down).start()
        for slot_at, slot in enumerate(slots):

            @pl.when(slot["is_relay"])
            def _():
                to_relay(kind, c, 0, slot_at, target).wait_recv()
                go_on(kind, c, x, slot_at, slot["dst"]).start()

    def gossip_end(kind, c):
        for q in range(4):
            direct(kind, c, q).wait_send()
        if kind == 1 and offset == 1:
            return
        if offset == 8:
            go_on(kind, c, 3, 0, down).wait_send()
        for slot_at, slot in enumerate(slots):

            @pl.when(slot["is_relay"])
            def _():
                go_on(kind, c, 0, slot_at, slot["dst"]).wait_send()

    for h in range(2):
        w_full[h, y, z] = w_low[:, own_columns(y, h * HALF, HALF)]
    for copy in own_copies[1:]:
        copy.wait()
    for c in range(first_early, CHUNKS):
        for q in range(4):
            go_send[c, q, 0] = w_low[:, part(q, c)]
            go_send[c, q, 1] = ma_ref[:, part(q, c)].astype(BF16)
            go_send[c, q, 2] = mb_ref[:, part(q, c)].astype(BF16)
            gossip_send(0, c, q)

    left = at_z(lax.rem(z + 3, 4))
    right = at_z(lax.rem(z + 1, 4))

    def pass_right(h, step):
        block = w_full.at[h, :, lax.rem(z + 4 - step, 4)]
        return remote(block, block, s_gz.at[h, 0, step], r_gz.at[h, 0, step], right)

    def pass_left(h, step):
        block = w_full.at[h, :, lax.rem(z + step, 4)]
        return remote(block, block, s_gz.at[h, 1, step], r_gz.at[h, 1, step], left)

    def gather_step(h, step):
        if step == 0:
            for copy in w_copies[h]:
                copy.wait_recv()
        else:

            @pl.when(z >= step)
            def _():
                pass_right(h, step - 1).wait_recv()

            @pl.when(z <= 3 - step)
            def _():
                pass_left(h, step - 1).wait_recv()

        if step < 3:

            @pl.when(jnp.logical_and(z >= step, z < 3))
            def _():
                pass_right(h, step).start()

            @pl.when(jnp.logical_and(z <= 3 - step, z > 0))
            def _():
                pass_left(h, step).start()

    def activations():
        for copy in acts_copies:
            copy.wait_recv()
        acts_t[...] = acts_in[...].T

    def sum_right(c, t):
        return remote(g_send.at[c, :, t], rs_in.at[0, c, t], s_rs.at[0, c, t], r_rs.at[0, c, t], right)

    def sum_left(c, t):
        return remote(g_send.at[c, :, t], rs_in.at[1, c, t], s_rs.at[1, c, t], r_rs.at[1, c, t], left)

    def straight(c, d):
        peer = xor(z, d)
        return remote(g_send.at[c, :, peer], rs_in.at[0, c, d], s_rs.at[0, c, d], r_rs.at[0, c, d], at_z(peer))

    def add_and_pass(c, t, way):
        copy = (sum_right, sum_left)[way](c, t)
        copy.wait_recv()
        g_send[c, :, t] = (g_send[c, :, t].astype(F32) + rs_in[way, c, t].astype(F32)).astype(BF16)
        copy.start()

    def pass_one(c):
        @pl.when(z == 1)
        def _():
            add_and_pass(c, 3, 0)
            add_and_pass(c, 2, 0)

        @pl.when(z == 2)
        def _():
            add_and_pass(c, 0, 1)
            add_and_pass(c, 1, 1)

    def pass_two(c):
        @pl.when(z == 2)
        def _():
            add_and_pass(c, 3, 0)

        @pl.when(z == 1)
        def _():
            add_and_pass(c, 0, 1)

    def gradient_chunk(c):
        for copy in cot_copies[c]:
            copy.wait_recv()
        result = jnp.dot(acts_t[...], cot_in[:, chunk(c)], preferred_element_type=F32)
        g_send[c] = (OUT_SCALE * result).astype(BF16).reshape(N_Y, N_Z, OWN, CW)
        if c >= first_straight:
            for d in (2, 3, 1):
                straight(c, d).start()
        else:

            @pl.when(z == 0)
            def _():
                for t in (3, 2, 1):
                    sum_right(c, t).start()

            @pl.when(z == 3)
            def _():
                for t in (0, 1, 2):
                    sum_left(c, t).start()

    gb_copies = [
        [
            remote(gb_send.at[c, xor(y, d)], gb_in.at[c, y], s_gb.at[c, d - 1], r_gb.at[c, d - 1], at_y(xor(y, d)))
            for d in (1, 2, 3)
        ]
        for c in range(CHUNKS)
    ]

    def reduce_chunk(c):
        if c >= first_straight:
            result = g_send[c, :, z].astype(F32)
            for d in (1, 2, 3):
                straight(c, d).wait_recv()
                result = result + rs_in[0, c, d].astype(F32)
            gb_send[c] = result.astype(BF16)
        else:
            total[...] = g_send[c, :, z].astype(F32)

            @pl.when(z > 0)
            def _():
                sum_right(c, z).wait_recv()
                total[...] += rs_in[0, c, z].astype(F32)

            @pl.when(z < 3)
            def _():
                sum_left(c, z).wait_recv()
                total[...] += rs_in[1, c, z].astype(F32)

            gb_send[c] = total[...].astype(BF16)
        for copy in gb_copies[c]:
            copy.start()
        gb_in[c, y] = gb_send[c, y]

    learn = par_ref[0]
    scale_one = par_ref[1]
    scale_two = par_ref[2]

    def adamw(weight, moment_a, moment_b, grad):
        a_up = BETA_ONE * moment_a + (1.0 - BETA_ONE) * grad
        b_up = BETA_TWO * moment_b + (1.0 - BETA_TWO) * grad * grad
        direction = a_up * scale_one / (jnp.sqrt(b_up * scale_two) + EPSILON) + DECAY * weight
        return weight - learn * direction, a_up, b_up

    def update_chunk(c):
        for copy in gb_copies[c]:
            copy.wait_recv()
        if c >= first_early:
            for q in range(4):
                gossip_send(1, c, q)
        for q in range(4):
            columns = part(q, c)
            w_up, a_up, b_up = adamw(
                w_ref[:, columns], ma_ref[:, columns], mb_ref[:, columns], gb_in[c, q].astype(F32)
            )
            if c < first_early:
                go_send[c, q, 0] = w_up.astype(BF16)
                go_send[c, q, 1] = a_up.astype(BF16)
                go_send[c, q, 2] = b_up.astype(BF16)
                gossip_send(0, c, q)
            w_out[:, columns] = 0.5 * w_up
            ma_out[:, columns] = 0.5 * a_up
            mb_out[:, columns] = 0.5 * b_up

    def mix_chunk(c):
        for q in range(4):
            direct(0, c, q).wait_recv()
            columns = part(q, c)
            w_up, a_up, b_up = (go_in[c, q, k].astype(F32) for k in range(3))
            if c >= first_early:
                direct(1, c, q).wait_recv()
                w_up, a_up, b_up = adamw(w_up, a_up, b_up, gg_in[c - first_early, q].astype(F32))
            w_out[:, columns] += 0.5 * w_up
            ma_out[:, columns] += 0.5 * a_up
            mb_out[:, columns] += 0.5 * b_up

    def product(d, h):
        return lax.dot_general(
            cot_in[tokens(d), pl.ds(h * HALF, HALF)],
            w_full[h].reshape(ROWS, HALF),
            (((1,), (1,)), ((), ())),
            preferred_element_type=F32,
        )

    def act_grad_start(d):
        ag_sum[d] = product(d, 0)

    ag_copies = [
        remote(ag_send.at[d - 1], ag_in.at[d - 1], s_ag.at[d - 1], r_ag.at[d - 1], at_y(xor(y, d)))
        for d in (1, 2, 3)
    ]

    def act_grad_send(d):
        ag_send[d - 1] = (ag_sum[d] + product(d, 1)).astype(BF16)
        ag_copies[d - 1].start()

    def act_grad_end():
        result = ag_sum[0] + product(0, 1)
        for d in (1, 2, 3):
            ag_copies[d - 1].wait_recv()
            result = result + ag_in[d - 1].astype(F32)
        ag_out[...] = (OUT_SCALE * result).astype(BF16)

    steps = [
        (8.0, gather_step, 0, 0),
        (9.5, gather_step, 1, 0),
        (12.5, gather_step, 0, 1),
        (15.5, gather_step, 1, 1),
        (16.0, activations),
        (17.5, gather_step, 0, 2),
        (20.5, gather_step, 1, 2),
        (22.0, gather_step, 0, 3),
        (26.5, gather_step, 1, 3),
        (23.5, act_grad_start, 0),
        (24.0, act_grad_start, 2),
        (25.0, act_grad_start, 1),
        (26.0, act_grad_start, 3),
        (29.3, act_grad_send, 2),
        (30.0, act_grad_send, 1),
        (30.7, act_grad_send, 3),
        (42.0, act_grad_end),
    ]
    for c in range(CHUNKS):
        at = 17.0 + 12.0 / CHUNKS * (c + 1)
        steps.append((at, gradient_chunk, c))
        if c >= first_straight:
            at += 5.0
        else:
            steps.append((at + 3.0, pass_one, c))
            steps.append((at + 5.5, pass_two, c))
            at += 8.0
        steps.append((at, reduce_chunk, c))
        at += 2.5
        steps.append((at, update_chunk, c))
        if c >= first_early:
            steps.append((16.2, relay_chunk, 0, c))
            steps.append((at + 3.0, relay_chunk, 1, c))
        else:
            steps.append((at + 4.0, relay_chunk, 0, c))
        steps.append((at + 8.0, mix_chunk, c))
    for _, act, *with_args in sorted(steps, key=lambda step: step[0]):
        act(*with_args)

    for copies in w_copies + [acts_copies, ag_copies] + cot_copies + gb_copies:
        for copy in copies:
            copy.wait_send()
    for h in range(2):
        for step in range(3):

            @pl.when(jnp.logical_and(z >= step, z < 3))
            def _():
                pass_right(h, step).wait_send()

            @pl.when(jnp.logical_and(z <= 3 - step, z > 0))
            def _():
                pass_left(h, step).wait_send()

    for c in range(CHUNKS):
        if c >= first_straight:
            for d in (1, 2, 3):
                straight(c, d).wait_send()
        else:
            for t in range(N_Z):

                @pl.when(z < t)
                def _():
                    sum_right(c, t).wait_send()

                @pl.when(z > t)
                def _():
                    sum_left(c, t).wait_send()

        gossip_end(0, c)
        if c >= first_early:
            gossip_end(1, c)


def step_kernel(offset, collective):
    n_slots = len(CROSSING.get(offset, ((0, None),)))
    early = max(EARLY[offset], 1)
    dma = pltpu.SemaphoreType.DMA
    vmem = pl.BlockSpec(memory_space=pltpu.VMEM)
    return pl.pallas_call(
        partial(gossip_kernel, offset),
        out_shape=(
            jax.ShapeDtypeStruct((TOK, ROWS), BF16),
            jax.ShapeDtypeStruct((OWN, D), F32),
            jax.ShapeDtypeStruct((OWN, D), F32),
            jax.ShapeDtypeStruct((OWN, D), F32),
        ),
        in_specs=[pl.BlockSpec(memory_space=pltpu.SMEM)] + [pl.BlockSpec(memory_space=pltpu.HBM)] * 5,
        out_specs=(vmem,) * 4,
        scratch_shapes=[pltpu.VMEM((OWN, D), F32)] * 3
        + [
            pltpu.VMEM((OWN, D), BF16),
            pltpu.VMEM((2, N_Y, N_Z, OWN, HALF), BF16),
            pltpu.VMEM((4 * TOK, ROWS), BF16),
            pltpu.VMEM((ROWS, 4 * TOK), BF16),
            pltpu.VMEM((4 * TOK, SLICE), BF16),
            pltpu.VMEM((CHUNKS, N_Y, N_Z, OWN, CW), BF16),
            pltpu.VMEM((2, CHUNKS, N_Z, N_Y, OWN, CW), BF16),
            pltpu.VMEM((N_Y, OWN, CW), F32),
            pltpu.VMEM((CHUNKS, N_Y, OWN, CW), BF16),
            pltpu.VMEM((CHUNKS, N_Y, OWN, CW), BF16),
            pltpu.VMEM((3, TOK, ROWS), BF16),
            pltpu.VMEM((3, TOK, ROWS), BF16),
            pltpu.VMEM((4, TOK, ROWS), F32),
            pltpu.VMEM((CHUNKS, 4, 3, OWN, CW), BF16),
            pltpu.VMEM((CHUNKS, 4, 3, OWN, CW), BF16),
            pltpu.VMEM((CHUNKS, n_slots, 3, OWN, CW), BF16),
            pltpu.VMEM((early, 4, OWN, CW), BF16),
            pltpu.VMEM((early, n_slots, OWN, CW), BF16),
            dma((2, 3)),
            dma((2, 3)),
            dma((3,)),
            dma((3,)),
            dma((CHUNKS, 3)),
            dma((CHUNKS, 3)),
            dma((2, 2, 3)),
            dma((2, 2, 3)),
            dma((2, CHUNKS, N_Z)),
            dma((2, CHUNKS, N_Z)),
            dma((CHUNKS, 3)),
            dma((CHUNKS, 3)),
            dma((3,)),
            dma((3,)),
            dma((CHUNKS, 4)),
            dma((CHUNKS, 4)),
            dma((CHUNKS, n_slots)),
            dma((CHUNKS, n_slots)),
            dma((early, 4)),
            dma((early, 4)),
            dma((early, n_slots)),
            dma((early, n_slots)),
            dma((5,)),
        ],
        compiler_params=pltpu.CompilerParams(
            collective_id=collective, has_side_effects=True, vmem_limit_bytes=58 << 20
        ),
        name="gossip_step_%d" % offset,
    )


def store_kernel(*refs):
    ins, outs, sems = refs[:4], refs[4:8], refs[8]
    copies = [pltpu.make_async_copy(src, dst, sems.at[i]) for i, (src, dst) in enumerate(zip(ins, outs))]
    for copy in copies:
        copy.start()
    for copy in copies:
        copy.wait()


def store(values):
    return pl.pallas_call(
        store_kernel,
        out_shape=tuple(jax.ShapeDtypeStruct(v.shape, v.dtype) for v in values),
        in_specs=[pl.BlockSpec(memory_space=pl.ANY)] * 4,
        out_specs=(pl.BlockSpec(memory_space=pltpu.HBM),) * 4,
        scratch_shapes=[pltpu.SemaphoreType.DMA((4,))],
        name="store_results",
    )(*values)


def local(acts, cotangent, weight, moment_one, moment_two, learn_rate, step_index, step_count):
    steps_float = step_count[0].astype(F32)
    fix_one = 1.0 - jnp.power(F32(BETA_ONE), steps_float)
    fix_two = 1.0 - jnp.power(F32(BETA_TWO), steps_float)
    numbers = jnp.stack([learn_rate[0], 1.0 / fix_one, 1.0 / fix_two])
    outs = lax.switch(
        step_index[0] % 4,
        [step_kernel(1 << level, level) for level in range(4)],
        numbers,
        acts[0],
        cotangent[0],
        weight[0],
        moment_one[0],
        moment_two[0],
    )
    return tuple(out[None] for out in store(outs))


def solution(mesh):
    split = P("rep", "fsdp", None)
    return jax.shard_map(
        local,
        mesh=mesh,
        in_specs=(split,) * 5 + (P(),) * 3,
        out_specs=(split,) * 4,
        check_vma=False,
    )
```

```python
from functools import partial

import jax
import jax.numpy as jnp
from jax import lax
from jax.experimental import pallas as pl
from jax.experimental.pallas import tpu as pltpu
from jax.sharding import PartitionSpec as P

BETA_ONE = 0.9
BETA_TWO = 0.95
EPSILON = 1e-08
DECAY = 0.1
OUT_SCALE = 0.015625

MESH = pl.DeviceIdType.MESH
F32 = jnp.float32
BF16 = jnp.bfloat16

N_Y = 4
N_Z = 4
TOK = 192
ROWS = 512
OWN = 32
D = 4096
SLICE = D // N_Y
CHUNKS = 4
CW = SLICE // CHUNKS
HALF = SLICE // 2

STRAIGHT = 1
EARLY = {1: 1, 2: 1, 4: 1, 8: 1}

CROSSING = {1: ((3, 1),), 2: ((3, None),), 4: ((2, None), (3, None))}


def xor(index, bits):
    low = lax.rem(index, 2)
    high = lax.div(index, 2)
    if bits & 1:
        low = 1 - low
    if bits & 2:
        high = 1 - high
    return high * 2 + low


def gossip_kernel(
    offset,
    par_ref,
    acts_ref,
    cot_ref,
    w_hbm,
    ma_hbm,
    mb_hbm,
    ag_out,
    w_out,
    ma_out,
    mb_out,
    w_ref,
    ma_ref,
    mb_ref,
    w_low,
    w_full,
    acts_in,
    acts_t,
    cot_in,
    g_send,
    rs_in,
    total,
    gb_send,
    gb_in,
    ag_send,
    ag_in,
    ag_sum,
    go_send,
    go_in,
    relay_in,
    gg_in,
    relay_gg,
    s_w,
    r_w,
    s_acts,
    r_acts,
    s_cot,
    r_cot,
    s_gz,
    r_gz,
    s_rs,
    r_rs,
    s_gb,
    r_gb,
    s_ag,
    r_ag,
    s_go,
    r_go,
    r_rel,
    s_fwd,
    s_gg,
    r_gg,
    r_relg,
    s_fwdg,
    s_own,
):
    rep = lax.axis_index("rep")
    fs = lax.axis_index("fsdp")
    zh = lax.div(rep, 8)
    xc = lax.rem(rep, 8)
    x = lax.div(xc, 2)
    core = lax.rem(rep, 2)
    y = lax.div(fs, N_Z)
    z = lax.rem(fs, N_Z)

    def at_y(value):
        return (rep, value * N_Z + z)

    def at_z(value):
        return (rep, y * N_Z + value)

    def remote(src, dst, send, recv, device):
        return pltpu.make_async_remote_copy(
            src_ref=src, dst_ref=dst, send_sem=send, recv_sem=recv, device_id=device, device_id_type=MESH
        )

    target = (lax.rem(rep + offset, 32), fs)
    source = (lax.rem(rep + 32 - offset, 32), fs)
    slots = []
    if offset == 8:
        z_all = zh * N_Z + z
        z_down = lax.rem(z_all + 10, 16)
        z_up = lax.rem(z_all + 6, 16)
        down = (lax.div(z_down, N_Z) * 8 + xc, y * N_Z + lax.rem(z_down, N_Z))
        up = (lax.div(z_up, N_Z) * 8 + xc, y * N_Z + lax.rem(z_up, N_Z))
    else:
        next_zh = lax.rem(zh + 1, 4)
        prev_zh = lax.rem(zh + 3, 4)
        for sx, sc in CROSSING[offset]:
            dx = ((sx * 2 + (sc or 0) + offset) % 8) // 2
            if sc is None:
                dc = core
                is_src = x == sx
                is_relay = x != sx
                is_dst = x == dx
                src_rep = zh * 8 + sx * 2 + core
            else:
                dc = 1 - sc
                is_src = jnp.logical_and(x == sx, core == sc)
                is_relay = jnp.logical_and(x != sx, core == dc)
                is_dst = jnp.logical_and(x == dx, core == dc)
                src_rep = zh * 8 + sx * 2 + sc
            slots.append(
                dict(
                    sx=sx,
                    is_src=is_src,
                    is_relay=is_relay,
                    is_dst=is_dst,
                    src=(src_rep, fs),
                    dst=(next_zh * 8 + dx * 2 + dc, fs),
                    relay=[(zh * 8 + q * 2 + dc, fs) for q in range(4)],
                    back=[(prev_zh * 8 + q * 2 + dc, fs) for q in range(4)],
                )
            )

    barrier = pltpu.get_barrier_semaphore()

    def greet(device):
        pl.semaphore_signal(barrier, inc=1, device_id=device, device_id_type=MESH)

    for d in (1, 2, 3):
        greet(at_y(xor(y, d)))
    for d in (1, 2, 3):
        greet(at_z(xor(z, d)))
    greet(source)
    expected = 7
    if offset == 8:
        greet(up)
        expected = 8
    for slot in slots:

        @pl.when(slot["is_relay"])
        def _():
            greet(slot["src"])

        @pl.when(slot["is_dst"])
        def _():
            for q in range(4):
                if q != slot["sx"]:
                    greet(slot["back"][q])

        expected = expected + slot["is_relay"].astype(jnp.int32) + 3 * slot["is_src"].astype(jnp.int32)

    early = EARLY[offset]
    first_early = CHUNKS - early
    first_straight = CHUNKS - STRAIGHT

    def part(q, c):
        return pl.ds(q * SLICE + c * CW, CW)

    def chunk(c):
        return pl.ds(c * CW, CW)

    def tokens(d):
        return pl.ds(d * TOK, TOK)

    own_cot = cot_ref.at[:, pl.ds(pl.multiple_of(y * SLICE, 128), SLICE)]
    own_copies = [
        pltpu.make_async_copy(src, dst, s_own.at[i])
        for i, (src, dst) in enumerate(
            (
                (w_hbm, w_ref),
                (acts_ref, acts_in.at[tokens(0)]),
                (own_cot, cot_in.at[tokens(0)]),
                (ma_hbm, ma_ref),
                (mb_hbm, mb_ref),
            )
        )
    ]
    for copy in own_copies:
        copy.start()
    own_copies[0].wait()
    w_low[...] = w_ref[...].astype(BF16)
    pl.semaphore_wait(barrier, expected)

    def own_columns(peer, start, width):
        return pl.ds(pl.multiple_of(peer * SLICE + start, 128), width)

    w_copies, acts_copies = [[], []], []
    cot_copies = [[] for _ in range(CHUNKS)]
    for d in (2, 1, 3):
        peer = xor(y, d)
        for h in range(2):
            w_copies[h].append(
                remote(
                    w_low.at[:, own_columns(peer, h * HALF, HALF)],
                    w_full.at[h, y, z],
                    s_w.at[h, d - 1],
                    r_w.at[h, d - 1],
                    at_y(peer),
                )
            )
        acts_copies.append(
            remote(acts_ref, acts_in.at[tokens(d)], s_acts.at[d - 1], r_acts.at[d - 1], at_y(peer))
        )
        for c in range(CHUNKS):
            cot_copies[c].append(
                remote(
                    cot_ref.at[:, own_columns(peer, c * CW, CW)],
                    cot_in.at[tokens(d), chunk(c)],
                    s_cot.at[c, d - 1],
                    r_cot.at[c, d - 1],
                    at_y(peer),
                )
            )
    for copy in w_copies[0] + w_copies[1] + acts_copies:
        copy.start()
    for c in range(CHUNKS):
        for copy in cot_copies[c]:
            copy.start()

    def ends(kind, c, q):
        if kind == 0:
            return go_send.at[c, q], go_in.at[c, q], s_go.at[c, q], r_go.at[c, q]
        e = c - first_early
        return gb_in.at[c, q], gg_in.at[e, q], s_gg.at[e, q], r_gg.at[e, q]

    def middle(kind, c, slot_at):
        if kind == 0:
            return relay_in.at[c, slot_at], r_rel.at[c, slot_at], s_fwd.at[c, slot_at]
        e = c - first_early
        return relay_gg.at[e, slot_at], r_relg.at[e, slot_at], s_fwdg.at[e, slot_at]

    def direct(kind, c, q):
        src, dst, send, recv = ends(kind, c, q)
        return remote(src, dst, send, recv, target)

    def to_relay(kind, c, q, slot_at, device):
        src, _, send, _ = ends(kind, c, q)
        hold, recv, _ = middle(kind, c, slot_at)
        return remote(src, hold, send, recv, device)

    def go_on(kind, c, q, slot_at, device):
        _, dst, _, recv = ends(kind, c, q)
        hold, _, send = middle(kind, c, slot_at)
        return remote(hold, dst, send, recv, device)

    def gossip_send(kind, c, q):
        if kind == 1 and offset == 1:
            direct(kind, c, q).start()
            return
        if offset == 8:
            if q < 3:
                direct(kind, c, q).start()
            else:
                to_relay(kind, c, q, 0, down).start()
            return
        by_relay = None
        for slot_at, slot in enumerate(slots):
            if q != slot["sx"]:

                @pl.when(slot["is_src"])
                def _():
                    to_relay(kind, c, q, slot_at, slot["relay"][q]).start()

                by_relay = slot["is_src"] if by_relay is None else jnp.logical_or(by_relay, slot["is_src"])
        if by_relay is None:
            direct(kind, c, q).start()
        else:

            @pl.when(jnp.logical_not(by_relay))
            def _():
                direct(kind, c, q).start()

    def relay_chunk(kind, c):
        if kind == 1 and offset == 1:
            return
        if offset == 8:
            to_relay(kind, c, 3, 0, down).wait_recv()
            go_on(kind, c, 3, 0, down).start()
        for slot_at, slot in enumerate(slots):

            @pl.when(slot["is_relay"])
            def _():
                to_relay(kind, c, 0, slot_at, target).wait_recv()
                go_on(kind, c, x, slot_at, slot["dst"]).start()

    def gossip_end(kind, c):
        for q in range(4):
            direct(kind, c, q).wait_send()
        if kind == 1 and offset == 1:
            return
        if offset == 8:
            go_on(kind, c, 3, 0, down).wait_send()
        for slot_at, slot in enumerate(slots):

            @pl.when(slot["is_relay"])
            def _():
                go_on(kind, c, 0, slot_at, slot["dst"]).wait_send()

    for h in range(2):
        w_full[h, y, z] = w_low[:, own_columns(y, h * HALF, HALF)]
    for copy in own_copies[1:]:
        copy.wait()
    for c in range(first_early, CHUNKS):
        for q in range(4):
            go_send[c, q, 0] = w_low[:, part(q, c)]
            go_send[c, q, 1] = ma_ref[:, part(q, c)].astype(BF16)
            go_send[c, q, 2] = mb_ref[:, part(q, c)].astype(BF16)
            gossip_send(0, c, q)

    left = at_z(lax.rem(z + 3, 4))
    right = at_z(lax.rem(z + 1, 4))

    def pass_right(h, step):
        block = w_full.at[h, :, lax.rem(z + 4 - step, 4)]
        return remote(block, block, s_gz.at[h, 0, step], r_gz.at[h, 0, step], right)

    def pass_left(h, step):
        block = w_full.at[h, :, lax.rem(z + step, 4)]
        return remote(block, block, s_gz.at[h, 1, step], r_gz.at[h, 1, step], left)

    def gather_step(h, step):
        if step == 0:
            for copy in w_copies[h]:
                copy.wait_recv()
        else:

            @pl.when(z >= step)
            def _():
                pass_right(h, step - 1).wait_recv()

            @pl.when(z <= 3 - step)
            def _():
                pass_left(h, step - 1).wait_recv()

        if step < 3:

            @pl.when(jnp.logical_and(z >= step, z < 3))
            def _():
                pass_right(h, step).start()

            @pl.when(jnp.logical_and(z <= 3 - step, z > 0))
            def _():
                pass_left(h, step).start()

    def activations():
        for copy in acts_copies:
            copy.wait_recv()
        acts_t[...] = acts_in[...].T

    def sum_right(c, t):
        return remote(g_send.at[c, :, t], rs_in.at[0, c, t], s_rs.at[0, c, t], r_rs.at[0, c, t], right)

    def sum_left(c, t):
        return remote(g_send.at[c, :, t], rs_in.at[1, c, t], s_rs.at[1, c, t], r_rs.at[1, c, t], left)

    def straight(c, d):
        peer = xor(z, d)
        return remote(g_send.at[c, :, peer], rs_in.at[0, c, d], s_rs.at[0, c, d], r_rs.at[0, c, d], at_z(peer))

    def add_and_pass(c, t, way):
        copy = (sum_right, sum_left)[way](c, t)
        copy.wait_recv()
        g_send[c, :, t] = (g_send[c, :, t].astype(F32) + rs_in[way, c, t].astype(F32)).astype(BF16)
        copy.start()

    def pass_one(c):
        @pl.when(z == 1)
        def _():
            add_and_pass(c, 3, 0)
            add_and_pass(c, 2, 0)

        @pl.when(z == 2)
        def _():
            add_and_pass(c, 0, 1)
            add_and_pass(c, 1, 1)

    def pass_two(c):
        @pl.when(z == 2)
        def _():
            add_and_pass(c, 3, 0)

        @pl.when(z == 1)
        def _():
            add_and_pass(c, 0, 1)

    def gradient_chunk(c):
        for copy in cot_copies[c]:
            copy.wait_recv()
        result = jnp.dot(acts_t[...], cot_in[:, chunk(c)], preferred_element_type=F32)
        g_send[c] = (OUT_SCALE * result).astype(BF16).reshape(N_Y, N_Z, OWN, CW)
        if c >= first_straight:
            for d in (2, 3, 1):
                straight(c, d).start()
        else:

            @pl.when(z == 0)
            def _():
                for t in (3, 2, 1):
                    sum_right(c, t).start()

            @pl.when(z == 3)
            def _():
                for t in (0, 1, 2):
                    sum_left(c, t).start()

    gb_copies = [
        [
            remote(gb_send.at[c, xor(y, d)], gb_in.at[c, y], s_gb.at[c, d - 1], r_gb.at[c, d - 1], at_y(xor(y, d)))
            for d in (1, 2, 3)
        ]
        for c in range(CHUNKS)
    ]

    def reduce_chunk(c):
        if c >= first_straight:
            result = g_send[c, :, z].astype(F32)
            for d in (1, 2, 3):
                straight(c, d).wait_recv()
                result = result + rs_in[0, c, d].astype(F32)
            gb_send[c] = result.astype(BF16)
        else:
            total[...] = g_send[c, :, z].astype(F32)

            @pl.when(z > 0)
            def _():
                sum_right(c, z).wait_recv()
                total[...] += rs_in[0, c, z].astype(F32)

            @pl.when(z < 3)
            def _():
                sum_left(c, z).wait_recv()
                total[...] += rs_in[1, c, z].astype(F32)

            gb_send[c] = total[...].astype(BF16)
        for copy in gb_copies[c]:
            copy.start()
        gb_in[c, y] = gb_send[c, y]

    learn = par_ref[0]
    scale_one = par_ref[1]
    scale_two = par_ref[2]

    def adamw(weight, moment_a, moment_b, grad):
        a_up = BETA_ONE * moment_a + (1.0 - BETA_ONE) * grad
        b_up = BETA_TWO * moment_b + (1.0 - BETA_TWO) * grad * grad
        direction = a_up * scale_one / (jnp.sqrt(b_up * scale_two) + EPSILON) + DECAY * weight
        return weight - learn * direction, a_up, b_up

    def update_chunk(c):
        for copy in gb_copies[c]:
            copy.wait_recv()
        if c >= first_early:
            for q in range(4):
                gossip_send(1, c, q)
        for q in range(4):
            columns = part(q, c)
            w_up, a_up, b_up = adamw(
                w_ref[:, columns], ma_ref[:, columns], mb_ref[:, columns], gb_in[c, q].astype(F32)
            )
            if c < first_early:
                go_send[c, q, 0] = w_up.astype(BF16)
                go_send[c, q, 1] = a_up.astype(BF16)
                go_send[c, q, 2] = b_up.astype(BF16)
                gossip_send(0, c, q)
            w_out[:, columns] = 0.5 * w_up
            ma_out[:, columns] = 0.5 * a_up
            mb_out[:, columns] = 0.5 * b_up

    def mix_chunk(c):
        for q in range(4):
            direct(0, c, q).wait_recv()
            columns = part(q, c)
            w_up, a_up, b_up = (go_in[c, q, k].astype(F32) for k in range(3))
            if c >= first_early:
                direct(1, c, q).wait_recv()
                w_up, a_up, b_up = adamw(w_up, a_up, b_up, gg_in[c - first_early, q].astype(F32))
            w_out[:, columns] += 0.5 * w_up
            ma_out[:, columns] += 0.5 * a_up
            mb_out[:, columns] += 0.5 * b_up

    def product(d, h):
        return lax.dot_general(
            cot_in[tokens(d), pl.ds(h * HALF, HALF)],
            w_full[h].reshape(ROWS, HALF),
            (((1,), (1,)), ((), ())),
            preferred_element_type=F32,
        )

    def act_grad_start(d):
        ag_sum[d] = product(d, 0)

    ag_copies = [
        remote(ag_send.at[d - 1], ag_in.at[d - 1], s_ag.at[d - 1], r_ag.at[d - 1], at_y(xor(y, d)))
        for d in (1, 2, 3)
    ]

    def act_grad_send(d):
        ag_send[d - 1] = (ag_sum[d] + product(d, 1)).astype(BF16)
        ag_copies[d - 1].start()

    def act_grad_end():
        result = ag_sum[0] + product(0, 1)
        for d in (1, 2, 3):
            ag_copies[d - 1].wait_recv()
            result = result + ag_in[d - 1].astype(F32)
        ag_out[...] = (OUT_SCALE * result).astype(BF16)

    steps = [
        (8.0, gather_step, 0, 0),
        (9.5, gather_step, 1, 0),
        (12.5, gather_step, 0, 1),
        (15.5, gather_step, 1, 1),
        (16.0, activations),
        (17.5, gather_step, 0, 2),
        (20.5, gather_step, 1, 2),
        (22.0, gather_step, 0, 3),
        (26.5, gather_step, 1, 3),
        (23.5, act_grad_start, 0),
        (24.0, act_grad_start, 2),
        (25.0, act_grad_start, 1),
        (26.0, act_grad_start, 3),
        (29.3, act_grad_send, 2),
        (30.0, act_grad_send, 1),
        (30.7, act_grad_send, 3),
        (42.0, act_grad_end),
    ]
    for c in range(CHUNKS):
        at = 17.0 + 12.0 / CHUNKS * (c + 1)
        steps.append((at, gradient_chunk, c))
        if c >= first_straight:
            at += 5.0
        else:
            steps.append((at + 3.0, pass_one, c))
            steps.append((at + 5.5, pass_two, c))
            at += 8.0
        steps.append((at, reduce_chunk, c))
        at += 2.5
        steps.append((at, update_chunk, c))
        if c >= first_early:
            steps.append((16.2, relay_chunk, 0, c))
            steps.append((at + 3.0, relay_chunk, 1, c))
        else:
            steps.append((at + 4.0, relay_chunk, 0, c))
        steps.append((at + 8.0, mix_chunk, c))
    for _, act, *with_args in sorted(steps, key=lambda step: step[0]):
        act(*with_args)

    for copies in w_copies + [acts_copies, ag_copies] + cot_copies + gb_copies:
        for copy in copies:
            copy.wait_send()
    for h in range(2):
        for step in range(3):

            @pl.when(jnp.logical_and(z >= step, z < 3))
            def _():
                pass_right(h, step).wait_send()

            @pl.when(jnp.logical_and(z <= 3 - step, z > 0))
            def _():
                pass_left(h, step).wait_send()

    for c in range(CHUNKS):
        if c >= first_straight:
            for d in (1, 2, 3):
                straight(c, d).wait_send()
        else:
            for t in range(N_Z):

                @pl.when(z < t)
                def _():
                    sum_right(c, t).wait_send()

                @pl.when(z > t)
                def _():
                    sum_left(c, t).wait_send()

        gossip_end(0, c)
        if c >= first_early:
            gossip_end(1, c)


def step_kernel(offset, collective):
    n_slots = len(CROSSING.get(offset, ((0, None),)))
    early = max(EARLY[offset], 1)
    dma = pltpu.SemaphoreType.DMA
    vmem = pl.BlockSpec(memory_space=pltpu.VMEM)
    return pl.pallas_call(
        partial(gossip_kernel, offset),
        out_shape=(
            jax.ShapeDtypeStruct((TOK, ROWS), BF16),
            jax.ShapeDtypeStruct((OWN, D), F32),
            jax.ShapeDtypeStruct((OWN, D), F32),
            jax.ShapeDtypeStruct((OWN, D), F32),
        ),
        in_specs=[pl.BlockSpec(memory_space=pltpu.SMEM)] + [pl.BlockSpec(memory_space=pltpu.HBM)] * 5,
        out_specs=(vmem,) * 4,
        scratch_shapes=[pltpu.VMEM((OWN, D), F32)] * 3
        + [
            pltpu.VMEM((OWN, D), BF16),
            pltpu.VMEM((2, N_Y, N_Z, OWN, HALF), BF16),
            pltpu.VMEM((4 * TOK, ROWS), BF16),
            pltpu.VMEM((ROWS, 4 * TOK), BF16),
            pltpu.VMEM((4 * TOK, SLICE), BF16),
            pltpu.VMEM((CHUNKS, N_Y, N_Z, OWN, CW), BF16),
            pltpu.VMEM((2, CHUNKS, N_Z, N_Y, OWN, CW), BF16),
            pltpu.VMEM((N_Y, OWN, CW), F32),
            pltpu.VMEM((CHUNKS, N_Y, OWN, CW), BF16),
            pltpu.VMEM((CHUNKS, N_Y, OWN, CW), BF16),
            pltpu.VMEM((3, TOK, ROWS), BF16),
            pltpu.VMEM((3, TOK, ROWS), BF16),
            pltpu.VMEM((4, TOK, ROWS), F32),
            pltpu.VMEM((CHUNKS, 4, 3, OWN, CW), BF16),
            pltpu.VMEM((CHUNKS, 4, 3, OWN, CW), BF16),
            pltpu.VMEM((CHUNKS, n_slots, 3, OWN, CW), BF16),
            pltpu.VMEM((early, 4, OWN, CW), BF16),
            pltpu.VMEM((early, n_slots, OWN, CW), BF16),
            dma((2, 3)),
            dma((2, 3)),
            dma((3,)),
            dma((3,)),
            dma((CHUNKS, 3)),
            dma((CHUNKS, 3)),
            dma((2, 2, 3)),
            dma((2, 2, 3)),
            dma((2, CHUNKS, N_Z)),
            dma((2, CHUNKS, N_Z)),
            dma((CHUNKS, 3)),
            dma((CHUNKS, 3)),
            dma((3,)),
            dma((3,)),
            dma((CHUNKS, 4)),
            dma((CHUNKS, 4)),
            dma((CHUNKS, n_slots)),
            dma((CHUNKS, n_slots)),
            dma((early, 4)),
            dma((early, 4)),
            dma((early, n_slots)),
            dma((early, n_slots)),
            dma((5,)),
        ],
        compiler_params=pltpu.CompilerParams(
            collective_id=collective, has_side_effects=True, vmem_limit_bytes=58 << 20
        ),
        name="gossip_step_%d" % offset,
    )


def store_kernel(*refs):
    ins, outs, sems = refs[:4], refs[4:8], refs[8]
    copies = [pltpu.make_async_copy(src, dst, sems.at[i]) for i, (src, dst) in enumerate(zip(ins, outs))]
    for copy in copies:
        copy.start()
    for copy in copies:
        copy.wait()


def store(values):
    return pl.pallas_call(
        store_kernel,
        out_shape=tuple(jax.ShapeDtypeStruct(v.shape, v.dtype) for v in values),
        in_specs=[pl.BlockSpec(memory_space=pl.ANY)] * 4,
        out_specs=(pl.BlockSpec(memory_space=pltpu.HBM),) * 4,
        scratch_shapes=[pltpu.SemaphoreType.DMA((4,))],
        name="store_results",
    )(*values)


def local(acts, cotangent, weight, moment_one, moment_two, learn_rate, step_index, step_count):
    steps_float = step_count[0].astype(F32)
    fix_one = 1.0 - jnp.power(F32(BETA_ONE), steps_float)
    fix_two = 1.0 - jnp.power(F32(BETA_TWO), steps_float)
    numbers = jnp.stack([learn_rate[0], 1.0 / fix_one, 1.0 / fix_two])
    outs = lax.switch(
        step_index[0] % 4,
        [step_kernel(1 << level, level) for level in range(4)],
        numbers,
        acts[0],
        cotangent[0],
        weight[0],
        moment_one[0],
        moment_two[0],
    )
    return tuple(out[None] for out in store(outs))


def solution(mesh):
    split = P("rep", "fsdp", None)
    return jax.shard_map(
        local,
        mesh=mesh,
        in_specs=(split,) * 5 + (P(),) * 3,
        out_specs=(split,) * 4,
        check_vma=False,
    )
```
